32 devices in a mesh: band: 8 (over z, x), samp: 4 (over y, core).
Axes of the slice: x: 2, y: 2, z: 4, core: 2. Of those that a mesh axis runs over, the one named last changes fastest.
Arguments:
- yearly_maps: bfloat16 [128, 48, 1440], P('samp', 'band'), may hold values from -8 to 8
- forcing_predictors: bfloat16 [128, 32], replicated, may hold values from -4 to 4
- ridge_strengths: float32 [8], replicated, may hold values from 32 to 512
- harmonic_tier_lookup: int32 [720], replicated, may hold values from 0 to 7
- east_west_wavecount: int32 [88], replicated, may hold values from 0 to 87, each once
- parallel_per_line: int32 [48], replicated, may hold values from 0 to 47, as said below
Outputs:
- resid_spec: bfloat16 [128, 88, 2, 720], P('samp', 'band')
- resid_grid: bfloat16 [128, 48, 1440], P('samp', 'band')
The draws below stay inside these ranges and needn't reach their ends.
Inputs may be any that keep to these rules, and one draw needn't show every extreme that they name: `harmonic_tier_lookup`: every level of 0 to 7 may occur. `east_west_wavecount`: a permutation of the wavenumbers 0 to 87. `parallel_per_line`: a permutation of the latitudes 0 to 47.
All inputs are finite; a program needn't handle non-finite values.
Results may differ from the reference program's by a relative error of at most 0.014.
Values may be sent and summed in bfloat16 or wider, within the bound.
A program may use at most 128 MiB of HBM per device.

```python
import math
import jax
import jax.numpy as jnp
from jax import lax

NLON = 1440
LDEG = 720
MSLOT = 11
P_SIZE = 32
SHRINKAGE_TIERS = 8
DEG_BLOCK = 24
S = 128
NLAT = 48
M = 88
N_BAND = 8


def latitude_order(key):
    return jax.random.permutation(jax.random.fold_in(key, 11), NLAT).astype(jnp.int32)


def turning_waves(key):
    latitude_rows = latitude_order(key)
    colatitude = math.pi * (latitude_rows.astype(jnp.float32) + 0.5) / NLAT
    turning = (LDEG - 0.5) * jnp.sin(colatitude)
    floored = jnp.floor(turning).astype(jnp.int32)
    offsets = jnp.arange(12, dtype=jnp.int32)
    waves = floored[:, None] + offsets[None, :]
    overshoot = waves.astype(jnp.float32) - turning[:, None]
    envelope = jnp.clip(overshoot, 0.0, 1.0) * jnp.clip((11.0 - overshoot) / 4.0, 0.0, 1.0)
    positions = jnp.arange(NLON, dtype=jnp.int32)
    turns = waves[:, :, None] * positions[None, None, :] % NLON
    angle = 2.0 * math.pi / NLON * turns.astype(jnp.float32)
    basis = jnp.stack([jnp.cos(angle), jnp.sin(angle)], axis=2)
    return basis * (0.15 * envelope)[:, :, None, None]


def joint_draw(key):
    folded = jax.random.fold_in(key, 7)
    key_cov = jax.random.fold_in(folded, 0)
    key_pattern = jax.random.fold_in(folded, 1)
    key_noise = jax.random.fold_in(folded, 2)
    key_wave = jax.random.fold_in(folded, 4)
    covariate_draw = jax.random.normal(key_cov, (S, P_SIZE), jnp.float32)
    noise = 0.5 * jax.random.normal(key_noise, (S, NLAT, NLON), jnp.float32)
    amplitude = jax.random.normal(key_wave, (S, NLAT, 12, 2), jnp.float32)
    covariate_draw = jnp.clip(covariate_draw, -4.0, 4.0)
    pattern = 0.15 * jax.random.normal(key_pattern, (P_SIZE, NLAT, NLON), jnp.float32)
    signal = jnp.einsum('sp,pjk->sjk', covariate_draw, pattern)
    edge_waves = jnp.einsum('sjdc,jdck->sjk', amplitude, turning_waves(key))
    return (covariate_draw, jnp.clip(signal + noise + edge_waves, -8.0, 8.0))


def draw_forcing_predictors(key, part):
    return joint_draw(key)[0].astype(jnp.bfloat16)


def draw_yearly_maps(key, part):
    return joint_draw(key)[1].astype(jnp.bfloat16)


def draw_parallel_per_line(key, part):
    return latitude_order(key)


def set_ends(values, rng, smallest, largest):
    longest = values.shape.index(max(values.shape))
    spots = []
    for shift in (0, 1):
        where = [jax.random.randint(jax.random.fold_in(rng, axis), (), 0, length) for axis, length in enumerate(values.shape)]
        where[longest] = (where[longest] + shift) % values.shape[longest]
        spots.append(tuple(where))
    return values.at[spots[0]].set(smallest).at[spots[1]].set(largest)


def setup_inputs(seed: int = 0) -> dict:
    streams_of = jax.random.split(jax.random.key(seed), 7)
    return {
        "yearly_maps": draw_yearly_maps(jax.random.fold_in(streams_of[6], 71), 0),
        "forcing_predictors": draw_forcing_predictors(jax.random.fold_in(streams_of[6], 71), 0),
        "ridge_strengths": jnp.clip(jnp.exp(jax.random.uniform(streams_of[2], (SHRINKAGE_TIERS,), jnp.float32, math.log(32.0), math.log(512.0))), 32.0, 512.0),
        "harmonic_tier_lookup": set_ends(jax.random.randint(streams_of[3], (LDEG,), 0, SHRINKAGE_TIERS), jax.random.fold_in(streams_of[3], 1), 0, SHRINKAGE_TIERS - 1).astype(jnp.int32),
        "east_west_wavecount": jax.random.permutation(streams_of[4], M).astype(jnp.int32),
        "parallel_per_line": draw_parallel_per_line(jax.random.fold_in(streams_of[6], 71), 0),
    }


highest = lax.Precision.HIGHEST
log_gamma_half = 0.5 * math.log(math.pi) - math.log(2.0)
rescale_limit = 1e+16
rescale_log = math.log(1e+16)

def widen(values):
    return lax.optimization_barrier(values).astype(jnp.float32)

def wave_table(waves, longitudes, scales):
    positions = jnp.arange(longitudes, dtype=jnp.int32)
    turns = positions[:, None] * waves[None, :] % longitudes
    angle = 2.0 * math.pi / longitudes * turns.astype(jnp.float32)
    columns = jnp.stack([jnp.cos(angle) * scales[None, :], jnp.sin(angle) * scales[None, :]], axis=2)
    return columns.reshape(longitudes, 2 * waves.shape[0]).astype(jnp.bfloat16)

def legendre_log_start(waves, colat):
    order = waves.astype(jnp.float32)[:, None]
    log_norm = 0.5 * math.log(0.5) + 0.5 * (lax.lgamma(order + 1.5) - log_gamma_half - lax.lgamma(order + 1.0))
    return log_norm + order * jnp.log(jnp.sin(colat))[None, :]

def legendre_block(carry_state, first, count, order, cosine):
    newer, older, log_scale = carry_state
    order_sq = order * order
    rows_out = []
    for step in range(count):
        degree = (first + step).astype(jnp.float32)
        degree_sq = degree * degree
        grow = jnp.sqrt(jnp.maximum(4.0 * degree_sq - 1.0, 1.0) / jnp.maximum(degree_sq - order_sq, 1.0))
        lower = degree - 1.0
        shrink = jnp.sqrt(jnp.maximum(lower * lower - order_sq, 0.0) / jnp.maximum(4.0 * lower * lower - 1.0, 1.0))
        advanced = grow * (cosine * newer - shrink * older)
        current = jnp.where(degree == order, jnp.ones_like(advanced), jnp.where(degree > order, advanced, jnp.zeros_like(advanced)))
        large_value = jnp.abs(current) > rescale_limit
        factor = jnp.where(large_value, 1.0 / rescale_limit, 1.0)
        log_scale = log_scale + jnp.where(large_value, rescale_log, 0.0)
        older = newer * factor
        newer = current * factor
        rows_out.append(newer * jnp.exp(log_scale))
    return ((newer, older, log_scale), jnp.stack(rows_out))

def analyse(spectra, waves, colat):
    order = waves.astype(jnp.float32)[:, None]
    cosine = jnp.cos(colat)[None, :]
    log_start = legendre_log_start(waves, colat)
    spectra_float = widen(spectra)

    def advance(carry_state, block):
        carry_state, rows_out = legendre_block(carry_state, block * DEG_BLOCK, DEG_BLOCK, order, cosine)
        table = widen(rows_out.astype(jnp.bfloat16))
        piece = jnp.einsum('dmj,smcj->smcd', table, spectra_float, precision=highest)
        return (carry_state, piece)
    blank = jnp.zeros_like(log_start)
    _, pieces = lax.scan(advance, (blank, blank, log_start), jnp.arange(LDEG // DEG_BLOCK, dtype=jnp.int32))
    return jnp.moveaxis(pieces, 0, 3).reshape(spectra.shape[0], spectra.shape[1], 2, LDEG)

def synthesise(coeffs, waves, colat):
    order = waves.astype(jnp.float32)[:, None]
    cosine = jnp.cos(colat)[None, :]
    log_start = legendre_log_start(waves, colat)
    coeffs_float = widen(coeffs)

    def advance(carry, block):
        carry_state, total = carry
        carry_state, rows_out = legendre_block(carry_state, block * DEG_BLOCK, DEG_BLOCK, order, cosine)
        table = widen(rows_out.astype(jnp.bfloat16))
        segment = lax.dynamic_slice_in_dim(coeffs_float, block * DEG_BLOCK, DEG_BLOCK, 3)
        total = total + jnp.einsum('dmj,pmcd->pmcj', table, segment, precision=highest)
        return ((carry_state, total), block)
    blank = jnp.zeros_like(log_start)
    empty = jnp.zeros((coeffs.shape[0], coeffs.shape[1], 2, colat.shape[0]), jnp.float32)
    final, _ = lax.scan(advance, ((blank, blank, log_start), empty), jnp.arange(LDEG // DEG_BLOCK, dtype=jnp.int32))
    return final[1]

def shrunken_reciprocals(second_moment_array, ridge_strengths):
    gram = jnp.dot(second_moment_array.T, second_moment_array, precision=highest)
    identity = jnp.eye(gram.shape[0], dtype=jnp.float32)

    def reciprocal_of_array(value):
        factor = jnp.linalg.cholesky(gram + value * identity)
        return jax.scipy.linalg.cho_solve((factor, True), identity)
    return lax.map(reciprocal_of_array, ridge_strengths)

def solve_degrees(reciprocal_arrays, index, cross):
    levels = jnp.arange(reciprocal_arrays.shape[0], dtype=jnp.int32)
    select = (index[:, None] == levels[None, :]).astype(jnp.float32)
    chosen = jnp.einsum('lk,kpq->lpq', select, reciprocal_arrays, precision=highest)
    return jnp.einsum('lpq,qmcl->pmcl', chosen, cross, precision=highest)

def reference(yearly_maps, forcing_predictors, ridge_strengths, harmonic_tier_lookup, east_west_wavecount, parallel_per_line):
    colat = math.pi * (parallel_per_line.astype(jnp.float32) + 0.5) / NLAT
    weight = math.pi / NLAT * jnp.sin(colat)
    second_moment_array = forcing_predictors.astype(jnp.float32)
    reciprocal_arrays = shrunken_reciprocals(second_moment_array, ridge_strengths)
    groups = east_west_wavecount.reshape(N_BAND, MSLOT)
    flat_fields = yearly_maps.reshape(S * NLAT, NLON)

    def per_group(waves):
        forward = wave_table(waves, NLON, jnp.ones((MSLOT,), jnp.float32))
        flat = jnp.dot(flat_fields.astype(jnp.float32), forward.astype(jnp.float32), preferred_element_type=jnp.float32)
        spectra = (flat.reshape(S, NLAT, 2 * MSLOT) * weight[None, :, None]).astype(jnp.bfloat16)
        spectra = jnp.transpose(spectra, (0, 2, 1)).reshape(S, MSLOT, 2, NLAT)
        coefficients = analyse(spectra, waves, colat)
        cross = jnp.einsum('sp,smcl->pmcl', second_moment_array, coefficients, precision=highest)
        pattern = solve_degrees(reciprocal_arrays, harmonic_tier_lookup, cross).astype(jnp.bfloat16)
        fitted_spec = jnp.einsum('sp,pmcl->smcl', second_moment_array, widen(pattern), precision=highest)
        residual = (coefficients - fitted_spec).astype(jnp.bfloat16)
        pattern_spectra = synthesise(pattern, waves, colat).astype(jnp.bfloat16)
        return (residual, pattern_spectra.reshape(P_SIZE, 2 * MSLOT, NLAT))
    resid_all, pattern_all = lax.map(per_group, groups)
    resid_spec = jnp.transpose(resid_all, (1, 0, 2, 3, 4)).reshape(S, M, 2, LDEG)
    pattern_full = jnp.transpose(pattern_all, (1, 0, 2, 3)).reshape(P_SIZE, 2 * M, NLAT)
    scales = jnp.where(east_west_wavecount == 0, 1.0, 2.0).astype(jnp.float32) / NLON
    backward = wave_table(east_west_wavecount, NLON, scales)
    pattern_grid = jnp.einsum('pnj,kn->pjk', widen(pattern_full), widen(backward), precision=highest).astype(jnp.bfloat16)
    grid_float = widen(pattern_grid)

    def per_field(pair):
        field, weights_row = pair
        fitted = jnp.einsum('p,pjk->jk', weights_row, grid_float, precision=highest)
        return (field.astype(jnp.float32) - fitted).astype(jnp.bfloat16)
    resid_grid = lax.map(per_field, (yearly_maps, second_moment_array))
    return (resid_spec, resid_grid)
```

```python
import functools
import math

import jax
import jax.numpy as jnp
import numpy as np
from jax import lax
from jax.experimental import pallas as pl
from jax.experimental.pallas import tpu as pltpu
from jax.sharding import PartitionSpec as P

highest = lax.Precision.HIGHEST
log_gamma_half = 0.5 * math.log(math.pi) - math.log(2.0)
rescale_limit = 1e16
rescale_log = math.log(1e16)


def wave_table(waves, longitudes, scales):
    positions = jnp.arange(longitudes, dtype=jnp.int32)
    turns = positions[:, None] * waves[None, :] % longitudes
    angle = 2.0 * math.pi / longitudes * turns.astype(jnp.float32)
    columns = jnp.stack(
        [jnp.cos(angle) * scales[None, :], jnp.sin(angle) * scales[None, :]], axis=2
    )
    return columns.reshape(longitudes, 2 * waves.shape[0]).astype(jnp.bfloat16)


def legendre_log_start(waves, colat):
    order = waves.astype(jnp.float32)[:, None]
    log_norm = 0.5 * math.log(0.5) + 0.5 * (
        lax.lgamma(order + 1.5) - log_gamma_half - lax.lgamma(order + 1.0)
    )
    return log_norm + order * jnp.log(jnp.sin(colat))[None, :]


STEPS = 8


def sweep_inverse(matrices):
    size = matrices.shape[-1]
    row_id = lax.broadcasted_iota(jnp.int32, matrices.shape, 1)
    col_id = lax.broadcasted_iota(jnp.int32, matrices.shape, 2)
    current = matrices
    for k in range(size):
        row = current[:, k : k + 1, :]
        col = current[:, :, k : k + 1]
        recip = 1.0 / current[:, k : k + 1, k : k + 1]
        scaled = row * recip
        swept = current - col * scaled
        swept = jnp.where(col_id == k, col * recip, swept)
        swept = jnp.where(row_id == k, jnp.where(col_id == k, -recip, scaled), swept)
        current = swept
    return -current


def table_kernel(slots, degrees, root_ref, rroot_ref, order_ref, cos_ref, log_ref, mat_ref, table_ref, inv_ref, rows_ref):
    inv_ref[...] = sweep_inverse(mat_ref[...])
    order = order_ref[...]
    cosine = cos_ref[...]
    order_sq = order * order
    lanes_rows = order.shape[0]

    def block(index, carry):
        newer, older, log_scale, shrink = carry
        for step in range(STEPS):
            place = index * STEPS + step
            degree = place.astype(jnp.float32)
            gap = degree * degree - order_sq
            held = jnp.maximum(gap, 1.0)
            inv_root = lax.rsqrt(held)
            inv_root = inv_root * (1.5 - 0.5 * held * inv_root * inv_root)
            grow = inv_root * root_ref[place]
            start = jnp.where(gap == 0.0, 1.0, 0.0)
            advanced = (grow * cosine) * newer + (start - (grow * shrink) * older)
            current = jnp.where(gap >= 0.0, advanced, 0.0)
            large_value = jnp.abs(current) > rescale_limit
            factor = jnp.where(large_value, 1.0 / rescale_limit, 1.0)
            log_scale = log_scale + jnp.where(large_value, rescale_log, 0.0)
            older = newer * factor
            newer = current * factor
            shrink = jnp.maximum(gap, 0.0) * inv_root * rroot_ref[place]
            values = newer * jnp.exp(log_scale)
            for tile in range(rows_ref.shape[0]):
                at = pl.ds(pl.multiple_of(place * lanes_rows, lanes_rows), lanes_rows)
                rows_ref[tile, at, :] = values[:, tile * 128 : (tile + 1) * 128]
        return newer, older, log_scale, shrink

    blank = jnp.zeros_like(order)
    lax.fori_loop(0, degrees // STEPS, block, (blank, blank, log_ref[...], blank))
    for slot in range(slots):
        for tile in range(table_ref.shape[2] // 128):
            cols = slice(tile * 128, (tile + 1) * 128)
            table_ref[slot, :, cols] = rows_ref[tile, pl.ds(slot % lanes_rows, degrees, stride=lanes_rows), :].astype(jnp.bfloat16)


def solve_kernel(first, offset, table_ref, spec_ref, cross_hi_ref, cross_lo_ref, w_hi_ref, w_lo_ref, cov_ref, tier_ref, resid_ref, back_ref):
    f32 = jnp.float32
    width = cross_hi_ref.shape[2]
    levels = w_hi_ref.shape[1] // width

    def one(slot, carry):
        table = table_ref[slot]
        cross = jnp.dot(table, cross_hi_ref[slot], preferred_element_type=f32)
        cross = cross + jnp.dot(table, cross_lo_ref[slot], preferred_element_type=f32)
        hi = cross.astype(jnp.bfloat16)
        lo = (cross - hi.astype(f32)).astype(jnp.bfloat16)
        every = jnp.dot(hi, w_hi_ref[...], preferred_element_type=f32)
        every = every + jnp.dot(lo, w_hi_ref[...], preferred_element_type=f32)
        every = every + jnp.dot(hi, w_lo_ref[...], preferred_element_type=f32)
        tier = tier_ref[...]
        lane_level = lax.broadcasted_iota(jnp.int32, tier.shape, 1) // width
        per_tile = 128 // width
        total = jnp.zeros(tier.shape, f32)
        for tile in range(levels // per_tile):
            piece = every[:, tile * 128 : (tile + 1) * 128]
            total = jnp.where(tier - tile * per_tile == lane_level, piece, total)
        merged = total[:, :width]
        for part in range(1, per_tile):
            merged = merged + total[:, part * width : (part + 1) * width]
        pattern = merged.astype(jnp.bfloat16)
        resid = jnp.dot(table, spec_ref[slot], preferred_element_type=f32)
        resid = resid - jnp.dot(pattern, cov_ref[...], preferred_element_type=f32)
        resid_ref[slot] = resid.T.astype(jnp.bfloat16)
        back = lax.dot_general(pattern, table, (((0,), (0,)), ((), ())), preferred_element_type=f32)
        rows = back_ref.shape[2]
        own = back[:, :rows]
        if offset + rows <= back.shape[1]:
            own = jnp.where(slot < first, own, back[:, offset : offset + rows])
        back_ref[slot] = own.astype(jnp.bfloat16)
        return carry

    lax.fori_loop(0, table_ref.shape[0], one, 0)


def local(
    yearly_maps,
    forcing_predictors,
    ridge_strengths,
    harmonic_tier_lookup,
    east_west_wavecount,
    parallel_per_line,
):
    f32, bf16 = jnp.float32, jnp.bfloat16
    band_index = lax.axis_index("band")
    samp_index = lax.axis_index("samp")
    bands = lax.axis_size("band")
    field_count, lat_rows, longitudes = yearly_maps.shape
    latitudes = parallel_per_line.shape[0]
    covariates = forcing_predictors.shape[1]
    degrees = harmonic_tier_lookup.shape[0]
    levels = ridge_strengths.shape[0]
    slots = east_west_wavecount.shape[0] // bands
    colat_all = math.pi * (parallel_per_line.astype(f32) + 0.5) / latitudes
    own_colat = lax.dynamic_slice_in_dim(colat_all, band_index * lat_rows, lat_rows)
    weight = math.pi / latitudes * jnp.sin(own_colat)
    unit_scale = jnp.ones(east_west_wavecount.shape, f32)
    forward = wave_table(east_west_wavecount, longitudes, unit_scale)
    spectra = jnp.einsum("slk,kn->snl", yearly_maps, forward, preferred_element_type=f32)
    spectra = (spectra * weight[None, None, :]).astype(bf16)
    own_waves = lax.dynamic_slice_in_dim(east_west_wavecount, band_index * slots, slots)
    block = lax.all_to_all(spectra, "band", split_axis=1, concat_axis=2, tiled=True)

    if latitudes <= 64:
        lane_width, groups, height = 64, 2, -(-slots // 16) * 8
    else:
        lane_width, groups, height = -(-latitudes // 128) * 128, 1, -(-slots // 8) * 8
    lanes = lane_width * groups
    first = min(height, slots)

    def packed(values, fill):
        values = jnp.pad(values, ((0, height * groups - slots), (0, lane_width - latitudes)), constant_values=fill)
        return values.reshape(groups, height, lane_width).transpose(1, 0, 2).reshape(height, lanes)

    log_start = legendre_log_start(own_waves, colat_all)
    order = packed(jnp.broadcast_to(own_waves.astype(f32)[:, None], log_start.shape), 0.0)
    cosine = packed(jnp.broadcast_to(jnp.cos(colat_all)[None, :], log_start.shape), 0.0)
    moment = forcing_predictors.astype(f32)
    gram = jnp.dot(moment.T, moment, precision=highest)
    matrices = gram[None] + ridge_strengths[:, None, None] * jnp.eye(covariates, dtype=f32)[None]
    degree = np.arange(degrees, dtype=np.float64)
    root = np.sqrt(np.maximum(4.0 * degree * degree - 1.0, 1.0))
    vmem = pl.BlockSpec(memory_space=pltpu.VMEM)
    smem = pl.BlockSpec(memory_space=pltpu.SMEM)
    table, inverse = pl.pallas_call(
        functools.partial(table_kernel, slots, degrees),
        out_shape=(
            jax.ShapeDtypeStruct((slots, degrees, lanes), bf16),
            jax.ShapeDtypeStruct((levels, covariates, covariates), f32),
        ),
        in_specs=[smem, smem, vmem, vmem, vmem, vmem],
        out_specs=(vmem, vmem),
        scratch_shapes=[pltpu.VMEM((lanes // 128, degrees * height, 128), f32)],
        compiler_params=pltpu.CompilerParams(vmem_limit_bytes=(16 if groups == 2 else 48) * 2**20),
        cost_estimate=pl.CostEstimate(flops=10**8, bytes_accessed=2 * 10**7, transcendentals=10**6),
        name="legendre_table",
    )(
        jnp.asarray(root.astype(np.float32)),
        jnp.asarray((1.0 / root).astype(np.float32)),
        order,
        cosine,
        packed(log_start, -1e4),
        matrices,
    )
    both = jnp.eye(2, dtype=f32)
    chosen = jnp.transpose(inverse, (2, 0, 1))
    chosen = (both[:, None, None, :, None] * chosen[None, :, :, None, :]).reshape(2 * covariates, levels * 2 * covariates)
    w_hi = chosen.astype(bf16)
    w_lo = (chosen - w_hi.astype(f32)).astype(bf16)
    own_cov = lax.dynamic_slice_in_dim(forcing_predictors, samp_index * field_count, field_count)
    cov_blocks = (both.astype(bf16)[:, None, :, None] * own_cov.T[None, :, None, :]).reshape(2 * covariates, 2 * field_count)

    block = block.reshape(field_count, slots, 2, latitudes).transpose(1, 3, 2, 0)
    own_cross = jnp.einsum("mjcs,sp->mjcp", block, own_cov, preferred_element_type=f32)
    cross = lax.psum(own_cross.reshape(slots, latitudes, 2 * covariates), "samp")

    def placed(values):
        low = jnp.pad(values[:first], ((0, 0), (0, lanes - latitudes), (0, 0)))
        if first == slots:
            return low
        high = jnp.pad(values[first:], ((0, 0), (lane_width, lane_width - latitudes), (0, 0)))
        return jnp.concatenate([low, high])

    cross_hi = cross.astype(bf16)
    cross_lo = (cross - cross_hi.astype(f32)).astype(bf16)
    tiers = jnp.broadcast_to(harmonic_tier_lookup[:, None], (degrees, 128))
    resid, back = pl.pallas_call(
        functools.partial(solve_kernel, first, lane_width),
        out_shape=(
            jax.ShapeDtypeStruct((slots, 2 * field_count, degrees), bf16),
            jax.ShapeDtypeStruct((slots, 2 * covariates, latitudes), bf16),
        ),
        in_specs=[vmem] * 8,
        out_specs=(vmem, vmem),
        compiler_params=pltpu.CompilerParams(vmem_limit_bytes=(16 if groups == 2 else 48) * 2**20),
        cost_estimate=pl.CostEstimate(flops=10**9, bytes_accessed=10**7, transcendentals=0),
        name="solve_degrees",
    )(table, placed(block.reshape(slots, latitudes, 2 * field_count)), placed(cross_hi), placed(cross_lo), w_hi, w_lo, cov_blocks, tiers)
    resid_spec = resid.reshape(slots, 2, field_count, degrees).transpose(2, 0, 1, 3)
    pattern_spectra = back.reshape(slots, 2, covariates, latitudes).transpose(2, 0, 1, 3)
    pattern_spectra = pattern_spectra.reshape(covariates, slots * 2, latitudes)
    returned = lax.all_to_all(pattern_spectra, "band", split_axis=2, concat_axis=1, tiled=True)
    late_waves, returned, own_maps = lax.optimization_barrier((east_west_wavecount, returned, yearly_maps))
    scales = jnp.where(late_waves == 0, 1.0, 2.0).astype(f32) / longitudes
    backward = wave_table(late_waves, longitudes, scales)
    grids = jnp.einsum("pnj,kn->pjk", returned, backward, preferred_element_type=f32).astype(bf16)
    fitted = jnp.einsum("sp,pjk->sjk", own_cov, grids, preferred_element_type=f32)
    resid_grid = (own_maps.astype(f32) - fitted).astype(bf16)
    return (resid_spec, resid_grid)


def solution(mesh):
    in_specs = (P("samp", "band", None), P(), P(), P(), P(), P())
    out_specs = (P("samp", "band", None, None), P("samp", "band", None))
    return jax.shard_map(local, mesh=mesh, in_specs=in_specs, out_specs=out_specs, check_vma=False)
```
